256 devices in a mesh: depth: 8 (over x, core), tile: 32 (over z, y).
Axes of the slice: x: 4, y: 4, z: 8, core: 2. Of those that a mesh axis runs over, the one named last changes fastest.
Arguments:
- volume: bfloat16 [4096, 64, 64, 64], P(('depth', 'tile')), may hold values from 0.0099487305 to 0.5
- resampler: bfloat16 [2, 64, 128], replicated, may hold values from 0 to 1.4, as said below
- ramp_slope: float32 [3], replicated, may hold values from -12 to 12
- ramp_pivot: float32 [3], replicated, may hold values from 0.03 to 0.3
- tile_owner: int32 [4096, 2], P(('depth', 'tile')), may hold values from 0 to 31, all different within a row; in each aligned block of 16 rows (0 to 15, 16 to 31, ...) at most 2 rows name the same one
- tile_cell: int32 [4096, 2], P(('depth', 'tile')), may hold values from 0 to 7
- depth_order: int32 [2, 4096], P(None, ('depth', 'tile')), may hold values from 0 to 4095, each once within a row
- slab_rank: int32 [2, 8], replicated, may hold values from 0 to 7, each once within a row
Outputs:
- colour: float32 [2, 3, 32, 512, 128], P(None, None, 'tile', 'depth')
- transmittance: float32 [2, 32, 512, 128], P(None, 'tile', 'depth')
The draws below stay inside these ranges and needn't reach their ends.
Inputs may be any that keep to these rules, and one draw needn't show every extreme that they name: `tile_owner`: each row names 2 different tile owners. Among the 16 rows of one device no owner is named by more than 2 rows, a bound that some block reaches. `depth_order`: each row is a permutation. `slab_rank`: each row is a permutation. `resampler`: nonnegative interpolation weights.
All inputs are finite; a program needn't handle non-finite values.
Results may differ from the reference program's by a relative error of at most 0.0025.
Values may be sent and summed in bfloat16 or wider, within the bound.
A program may use at most 128 MiB of HBM per device.

```python
import math
import jax
import jax.numpy as jnp
import numpy as np
from jax import lax

BRICK = 64
SAMPLES = 128
CELLS = 8
VIEWS = 2
BRICKS_DEV = 16
TILES = 32
SLABS = 8
BRICKS = 4096
CAP = 2


def draw_resampler(key, part):
    subkeys = jax.random.split(key, 2)
    shear_offset = jax.random.uniform(subkeys[0], (VIEWS, 1, 1), minval=-0.5, maxval=0.5)
    jitter = 0.25
    roughness = jax.random.uniform(subkeys[1], (VIEWS, BRICK, SAMPLES), minval=-1.0, maxval=1.0)
    voxel_pos = jnp.arange(BRICK, dtype=jnp.float32)[None, :, None]
    sample_pos = (jnp.arange(SAMPLES, dtype=jnp.float32)[None, None, :] + 0.5) * (BRICK / SAMPLES) - 0.5 + shear_offset
    tent_weight = jnp.maximum(0.0, 1.0 - jnp.abs(voxel_pos - sample_pos))
    return (tent_weight * (1.0 + jitter * roughness)).astype(jnp.bfloat16)


def touch_ends(drawn, stream_key, least, largest):
    shape = drawn.shape
    index_at = [jax.random.randint(jax.random.fold_in(stream_key, axis), (), 0, shape[axis]) for axis in range(len(shape))]
    drawn = drawn.at[tuple(index_at)].set(least)
    longest = shape.index(max(shape))
    index_at[longest] = (index_at[longest] + 1) % shape[longest]
    return drawn.at[tuple(index_at)].set(largest)


def shard_levels(stream_key, dims, cuts, smallest, high):
    def one(position, parts):
        heights = jax.random.uniform(jax.random.fold_in(jax.random.fold_in(stream_key, 6), position), (parts,), jnp.float32, smallest / len(cuts), high / len(cuts))
        return jnp.repeat(jnp.exp(heights), dims[position] // parts).reshape((-1,) + (1,) * (len(dims) - position - 1))

    gain = one(*cuts[0])
    for cut in cuts[1:]:
        gain = gain * one(*cut)
    return gain


def shared_out(own_key, own, number, rows, count, top, bound, skew):
    sequence = jax.random.permutation(own_key, count)
    heavy_load, common = shares(count, rows * top, bound, skew, True), shares(count, rows * top, bound, skew, False)
    places = jnp.arange(count)

    def named(tallies, rotation):
        used = int((tallies > 0).sum())
        fixed = max(1, used // 4)
        shifted = fixed + (places - fixed + rotation * (used - fixed)) % max(1, count - fixed)
        return jnp.zeros((count,), jnp.int32).at[sequence[jnp.where(places < fixed, places, shifted)]].set(jnp.asarray(tallies, jnp.int32))

    tallies = jnp.where(number % 4 == 0, named(heavy_load, number // 4), named(common, number - number // 4 - 1))
    mixed = jax.random.permutation(jax.random.fold_in(own, 3), count)
    source_of, taker = mixed[0:count // 2 * 2:2], mixed[1:count // 2 * 2:2]
    slack = jnp.minimum(tallies[source_of] - 1, bound - tallies[taker]) // 2
    slack = jnp.where((source_of == sequence[0]) | (taker == sequence[0]) | (tallies[taker] == 0), 0, jnp.maximum(slack, 0))
    shifted = jax.random.randint(jax.random.fold_in(own, 4), (count // 2,), 0, 1 << 20) % (slack + 1)
    tallies = tallies.at[source_of].add(-shifted).at[taker].add(shifted)
    items = jnp.searchsorted(jnp.cumsum(tallies), jnp.arange(rows * top), side="right").astype(jnp.int32)
    table = items.reshape(top, rows).T
    table = table[jax.random.permutation(jax.random.fold_in(own, 1), rows)]
    rotation = jax.random.randint(jax.random.fold_in(own, 2), (rows, 1), 0, top)
    return jnp.take_along_axis(table, (jnp.arange(top)[None, :] + rotation) % top, axis=1)


def shares(amount, total, reach, slope, full):
    portions = [(1 << 20) // math.isqrt(standing ** slope) + 1 for standing in range(1, amount + 1)]
    largest = reach if full else min(reach, max(-(-total // amount), total * portions[0] // sum(portions)))
    least = 1 if total - largest >= amount - 1 else 0
    given, rest = [largest] + [least] * (amount - 1), total - largest - least * (amount - 1)
    while rest > 0:
        candidates = [i for i in range(1, amount) if given[i] < largest] or [i for i in range(1, amount) if given[i] < reach]
        mass, remaining = sum([portions[i] for i in candidates]), rest
        for i in candidates:
            more = min(reach - given[i], max(1, remaining * portions[i] // mass), rest)
            given[i] = given[i] + more
            rest = rest - more
    return np.array(given)


def setup_inputs(seed: int = 0) -> dict:
    splits = jax.random.split(jax.random.key(seed), 9)
    volume = jnp.clip(jnp.exp(math.log(0.5) - 3.9171631 * jax.random.uniform(splits[0], (BRICKS, BRICK, BRICK, BRICK), jnp.float32) ** shard_levels(splits[0], (BRICKS, BRICK, BRICK, BRICK), ((0, 256),), -0.2, 0.2)), 0.0099487305, 0.5).astype(jnp.bfloat16)
    resampler = draw_resampler(jax.random.fold_in(splits[8], 71), 0)
    ramp_slope = jnp.clip(jax.random.uniform(splits[2], (3,), jnp.float32, -12.0, 12.0), -12.0, 12.0)
    ramp_pivot = jnp.clip(jax.random.uniform(splits[3], (3,), jnp.float32, 0.03, 0.3), 0.03, 0.3)
    tile_owner_keys = jax.random.split(jax.random.fold_in(splits[4], 1), BRICKS // BRICKS_DEV)
    tile_owner_turns = jax.random.permutation(jax.random.fold_in(splits[4], 3), BRICKS // BRICKS_DEV)
    tile_owner = jax.vmap(lambda own, number: shared_out(jax.random.fold_in(splits[4], 2), own, number, BRICKS_DEV, TILES, VIEWS, CAP, 2))(tile_owner_keys, tile_owner_turns).reshape((BRICKS, VIEWS))
    tile_cell = touch_ends(jax.random.randint(splits[5], (BRICKS, VIEWS), 0, CELLS), jax.random.fold_in(splits[5], 1), 0, CELLS - 1).astype(jnp.int32)
    depth_order = jax.vmap(lambda own: jax.random.permutation(own, BRICKS))(jax.random.split(splits[6], VIEWS)).reshape((VIEWS, BRICKS)).astype(jnp.int32)
    slab_rank = jax.vmap(lambda own: jax.random.permutation(own, SLABS))(jax.random.split(splits[7], VIEWS)).reshape((VIEWS, SLABS)).astype(jnp.int32)
    return dict(volume=volume, resampler=resampler, ramp_slope=ramp_slope, ramp_pivot=ramp_pivot, tile_owner=tile_owner, tile_cell=tile_cell, depth_order=depth_order, slab_rank=slab_rank)


EXTINCTION = 1.0
TOP_PRECISION = lax.Precision.HIGHEST


def render_brick(brick, resampler, ramp_slope, ramp_pivot):
    cube = brick.astype(jnp.float32)
    weights = resampler.astype(jnp.float32)
    rowwise_axis = jnp.einsum("kri,is->krs", cube, weights[0], precision=TOP_PRECISION)
    along_depth = jnp.einsum("rik,is->krs", cube, weights[1], precision=TOP_PRECISION)
    samples = jnp.stack([rowwise_axis, along_depth])
    optical = samples * (EXTINCTION / samples.shape[1])
    nearest_depth = jnp.cumsum(optical, axis=1) - optical
    weight = jnp.exp(-nearest_depth) * (1.0 - jnp.exp(-optical))
    layers = []
    for channel in range(3):
        tinted = jax.nn.sigmoid(ramp_slope[channel] * (samples - ramp_pivot[channel]))
        layers.append(jnp.sum(weight * tinted, axis=1))
    layers.append(jnp.sum(optical, axis=1))
    return jnp.stack(layers, axis=1)


def compose_slab(prints, owners, cells, ranks):
    tiles_out = []
    for view_index in range(2):
        flat_prints = prints[:, view_index]
        brick_count = flat_prints.shape[0]
        target = owners[:, view_index] * CELLS + cells[:, view_index]
        rank_tag = ranks[view_index]
        before = (target[None, :] == target[:, None]) & (rank_tag[None, :] < rank_tag[:, None])
        depth_values = flat_prints[:, 3].reshape(brick_count, -1)
        nearest_depth = jnp.dot(before.astype(jnp.float32), depth_values, precision=TOP_PRECISION)
        nearest_depth = nearest_depth.reshape(flat_prints[:, 3].shape)
        lit_colour = flat_prints[:, :3] * jnp.exp(-nearest_depth)[:, None]
        combined_result = jnp.concatenate([lit_colour, flat_prints[:, 3:]], axis=1)
        summed = jax.ops.segment_sum(combined_result, target, num_segments=TILES * CELLS)
        summed = summed.reshape(TILES, CELLS, 4, BRICK, SAMPLES).transpose(0, 2, 1, 3, 4)
        tiles_out.append(summed.reshape(TILES, 4, CELLS * BRICK, SAMPLES))
    return jnp.stack(tiles_out).astype(jnp.bfloat16)


def reference(volume, resampler, ramp_slope, ramp_pivot, tile_owner, tile_cell, depth_order, slab_rank):
    slab_bricks = BRICKS_DEV * TILES

    def one_slab(slab):
        start = (slab * slab_bricks).astype(jnp.int32)
        cubes = lax.dynamic_slice_in_dim(volume, start, slab_bricks, 0)
        owners = lax.dynamic_slice_in_dim(tile_owner, start, slab_bricks, 0)
        cells = lax.dynamic_slice_in_dim(tile_cell, start, slab_bricks, 0)
        ranks = lax.dynamic_slice_in_dim(depth_order, start, slab_bricks, 1)
        prints = lax.map(lambda brick: render_brick(brick, resampler, ramp_slope, ramp_pivot), cubes)
        return compose_slab(prints, owners, cells, ranks)

    slab_tiles = lax.map(one_slab, jnp.arange(SLABS, dtype=jnp.int32)).astype(jnp.float32)
    is_nearer = (slab_rank[:, None, :] < slab_rank[:, :, None]).astype(jnp.float32)
    depth_values = slab_tiles[:, :, :, 3]
    nearest_depth = jnp.einsum("jeh,hjxqg->ejxqg", is_nearer, depth_values, precision=TOP_PRECISION)
    colour = jnp.sum(jnp.exp(-nearest_depth)[:, :, :, None] * slab_tiles[:, :, :, :3], axis=0)
    colour = colour.transpose(0, 2, 1, 3, 4)
    transmittance = jnp.exp(-jnp.sum(depth_values, axis=0))
    return (colour, transmittance)
```

```python
import jax
import jax.numpy as jnp
from jax import lax
from jax.experimental import pallas as pl
from jax.experimental.pallas import tpu as pltpu
from jax.sharding import PartitionSpec as P

BF = jnp.bfloat16
F32 = jnp.float32
CELLS = 8
ROWS = 64
COLS = 128
BRICKS = 16
OWNERS = 32
SLOTS = 64
RC = 16
CHUNKS = ROWS // RC
EXP_SCALE = -1.4426950408889634 / 64.0


def march(samples_of, coef, write):
    zero = jnp.zeros((RC, COLS), F32)

    def step(block, carry):
        front, light, a0, a1, a2 = carry
        acc = [a0, a1, a2]
        rows = samples_of(block)
        for j in range(8):
            s = rows[j]
            front = front + s
            after = jnp.exp2(front * EXP_SCALE)
            weight = light - after
            light = after
            for c in range(3):
                acc[c] = acc[c] + weight * jnp.tanh(s * coef[c][0] + coef[c][1])
        return (front, light, *acc)

    front, light, a0, a1, a2 = lax.fori_loop(0, 8, step, (zero, zero + 1.0, zero, zero, zero), unroll=8)
    total = 1.0 - light
    for c, acc in enumerate((a0, a1, a2)):
        write(c, (0.5 * (total + acc)).astype(BF))
    write(3, (front * (1.0 / 64.0)).astype(BF))


def render_kernel(place, slope, pivot, res0, res1, vol0, vol1, out, samples):
    coef = []
    for c in range(3):
        half = slope[c] * 0.5
        coef.append((half, -half * pivot[c]))
    brick = pl.program_id(0)

    def samples0(block):
        x = vol0[0, pl.ds(block * 8, 8)].reshape(8 * RC, ROWS)
        return jnp.dot(x, res0[...], preferred_element_type=F32).reshape(8, RC, COLS)

    slot0 = place[2 * brick]
    slot1 = place[2 * brick + 1]

    def write0(c, x):
        out[slot0, c] = x

    def write1(c, x):
        out[slot1, c] = x

    march(samples0, coef, write0)
    half = RC // 2
    for r in range(half):
        x = jnp.concatenate([vol1[0, r], vol1[0, r + half]], axis=0)
        y = lax.dot_general(x, res1[...], (((0,), (0,)), ((), ())), preferred_element_type=F32)
        samples[pl.ds(r, 64, stride=RC), :] = y[:, :COLS]
        samples[pl.ds(r + half, 64, stride=RC), :] = y[:, COLS:]

    def samples1(block):
        return samples[pl.ds(block * 8 * RC, 8 * RC), :].reshape(8, RC, COLS)

    march(samples1, coef, write1)


def render(chunk, place, slope, pivot, res0, res1, volume):
    smem = pl.BlockSpec(memory_space=pltpu.SMEM)
    return pl.pallas_call(
        render_kernel,
        grid=(BRICKS,),
        in_specs=[
            smem,
            smem,
            smem,
            pl.BlockSpec((64, COLS), lambda b: (0, 0)),
            pl.BlockSpec((128, 2 * COLS), lambda b: (0, 0)),
            pl.BlockSpec((1, 64, RC, 64), lambda b: (b, 0, chunk, 0)),
            pl.BlockSpec((1, RC, 64, 64), lambda b: (b, chunk, 0, 0)),
        ],
        out_specs=pl.BlockSpec((SLOTS, 4, RC, COLS), lambda b: (0, 0, 0, 0)),
        out_shape=jax.ShapeDtypeStruct((SLOTS, 4, RC, COLS), BF),
        scratch_shapes=[pltpu.VMEM((64 * RC, COLS), F32)],
        compiler_params=pltpu.CompilerParams(vmem_limit_bytes=32 << 20),
        cost_estimate=pl.CostEstimate(flops=40_000_000_000, bytes_accessed=10_000_000, transcendentals=16_000_000),
        name=f"render{chunk}",
    )(place, slope, pivot, res0, res1, volume, volume)


def compose_kernel(count, order, target, received, out, acc):
    acc[...] = jnp.zeros_like(acc)

    def step(i, _):
        slot = order[i]
        t = target[i]
        x = received[slot].astype(F32)
        inner = acc[t, 3]
        shade = jnp.exp(-inner)
        for c in range(3):
            acc[t, c] = acc[t, c] + x[c] * shade
        acc[t, 3] = inner + x[3]
        return 0

    lax.fori_loop(0, count[0], step, 0)
    out[...] = acc[...].astype(BF)


def compose(chunk, count, order, target, received):
    smem = pl.BlockSpec(memory_space=pltpu.SMEM)
    vmem = pl.BlockSpec(memory_space=pltpu.VMEM)
    return pl.pallas_call(
        compose_kernel,
        in_specs=[smem, smem, smem, vmem],
        out_specs=vmem,
        out_shape=jax.ShapeDtypeStruct((2 * CELLS, 4, RC, COLS), BF),
        scratch_shapes=[pltpu.VMEM((2 * CELLS, 4, RC, COLS), F32)],
        compiler_params=pltpu.CompilerParams(vmem_limit_bytes=32 << 20),
        cost_estimate=pl.CostEstimate(flops=4_000_000, bytes_accessed=1_500_000, transcendentals=200_000),
        name=f"compose{chunk}",
    )(count, order, target, received)


def blend_kernel(chain, *refs):
    bands, (colour, light_out) = refs[:CHUNKS], refs[CHUNKS:]
    for view in range(2):
        for k in range(CHUNKS):
            rows = pl.ds(k * RC, RC)
            front = jnp.zeros((RC, COLS), F32)
            acc = [jnp.zeros((RC, COLS), F32)] * 3
            for j in range(8):
                x = bands[k][chain[view * 8 + j] * 2 + view].astype(F32)
                shade = jnp.exp(-front)
                for c in range(3):
                    acc[c] = acc[c] + shade * x[c]
                front = front + x[3]
            for c in range(3):
                colour[view, c, 0, rows, :] = acc[c]
            light_out[view, 0, rows, :] = jnp.exp(-front)


def blend(chain, bands):
    smem = pl.BlockSpec(memory_space=pltpu.SMEM)
    vmem = pl.BlockSpec(memory_space=pltpu.VMEM)
    return pl.pallas_call(
        blend_kernel,
        in_specs=[smem] + [vmem] * CHUNKS,
        out_specs=[vmem, vmem],
        out_shape=[
            jax.ShapeDtypeStruct((2, 3, 1, ROWS, COLS), F32),
            jax.ShapeDtypeStruct((2, 1, ROWS, COLS), F32),
        ],
        compiler_params=pltpu.CompilerParams(vmem_limit_bytes=32 << 20),
        name="blend",
    )(chain, *bands)


def body(volume, resampler, slope, pivot, tile_owner, tile_cell, depth_order, slab_rank):
    ids = jnp.arange(32)
    owner = tile_owner.reshape(-1)
    same = (owner[None, :] == owner[:, None]) & (ids[None, :] < ids[:, None])
    place = owner * 2 + jnp.sum(same.astype(jnp.int32), axis=1)
    view = jnp.tile(jnp.arange(2, dtype=jnp.int32), BRICKS)
    tag = depth_order.T.reshape(-1) * 16 + tile_cell.reshape(-1) * 2 + view
    hit = place[None, :] == jnp.arange(SLOTS, dtype=jnp.int32)[:, None]
    empty = 1 << 20
    slot_tag = jnp.min(jnp.where(hit, tag[None, :], empty), axis=1)
    tags = lax.all_to_all(slot_tag.reshape(OWNERS, 2), "tile", split_axis=0, concat_axis=0, tiled=True).reshape(-1)
    filled = tags < empty
    slots = jnp.arange(SLOTS, dtype=jnp.int32)
    before = (tags[None, :] < tags[:, None]) | ((tags[None, :] == tags[:, None]) & (slots[None, :] < slots[:, None]))
    position = jnp.sum(before.astype(jnp.int32), axis=1)
    at = position[None, :] == slots[:, None]
    order = jnp.sum(jnp.where(at, slots[None, :], 0), axis=1)
    target = jnp.sum(jnp.where(at, jnp.where(filled, tags % 16, 0)[None, :], 0), axis=1)
    count = jnp.sum(filled.astype(jnp.int32)).reshape(1)
    slabs = jnp.arange(8, dtype=jnp.int32)
    chain = jnp.sum(
        jnp.where(slab_rank[:, None, :] == slabs[None, :, None], slabs[None, None, :], 0), axis=2
    ).reshape(-1)
    res0 = resampler[0]
    zero = jnp.zeros_like(res0)
    res1 = jnp.concatenate(
        [jnp.concatenate([resampler[1], zero], 1), jnp.concatenate([zero, resampler[1]], 1)], 0
    )
    bands = []
    for k in range(CHUNKS):
        sent = render(k, place, slope, pivot, res0, res1, volume)
        got = lax.all_to_all(sent.reshape(OWNERS, 2, 4, RC, COLS), "tile", split_axis=0, concat_axis=0, tiled=True)
        piece = compose(k, count, order, target, got.reshape(SLOTS, 4, RC, COLS))
        bands.append(
            lax.all_to_all(piece.reshape(8, 2, 4, RC, COLS), "depth", split_axis=0, concat_axis=0, tiled=True).reshape(
                16, 4, RC, COLS
            )
        )
    return tuple(blend(chain, bands))


def solution(mesh):
    in_specs = (
        P(("depth", "tile"), None, None, None),
        P(),
        P(),
        P(),
        P(("depth", "tile"), None),
        P(("depth", "tile"), None),
        P(None, ("depth", "tile")),
        P(),
    )
    out_specs = (P(None, None, "tile", "depth", None), P(None, "tile", "depth", None))
    return jax.shard_map(body, mesh=mesh, in_specs=in_specs, out_specs=out_specs, check_vma=False)
```

```python
import jax
import jax.numpy as jnp
from jax import lax
from jax.experimental import pallas as pl
from jax.experimental.pallas import tpu as pltpu
from jax.sharding import PartitionSpec as P

BF = jnp.bfloat16
F32 = jnp.float32
I32 = jnp.int32
MESH = pl.DeviceIdType.MESH
ROWS = 64
COLS = 128
BRICKS = 16
ITEMS = 2 * BRICKS
NZ, NY = 8, 4
OWNERS = NZ * NY
SLABS = 8
SLOTS = 64
TARGETS = 16
RC = 16
CHUNKS = ROWS // RC
EMPTY = 1 << 20
EXP_SCALE = -1.4426950408889634 / 64.0


def march(samples_of, coef, write):
    zero = jnp.zeros((RC, COLS), F32)

    def step(block, carry):
        front, light, a0, a1, a2 = carry
        acc = [a0, a1, a2]
        rows = samples_of(block)
        for j in range(8):
            s = rows[j]
            front = front + s
            after = jnp.exp2(front * EXP_SCALE)
            weight = light - after
            light = after
            for c in range(3):
                acc[c] = acc[c] + weight * jnp.tanh(s * coef[c][0] + coef[c][1])
        return (front, light, *acc)

    front, light, a0, a1, a2 = lax.fori_loop(0, 8, step, (zero, zero + 1.0, zero, zero, zero), unroll=8)
    total = 1.0 - light
    for c, acc in enumerate((a0, a1, a2)):
        write(c, (0.5 * (total + acc)).astype(BF))
    write(3, (front * (1.0 / 64.0)).astype(BF))


def render_rows(brick, chunk, coef, res0, res1, bricks, samples, prints):
    top = pl.multiple_of(chunk * RC, RC)

    def samples0(block):
        x = bricks[brick, pl.ds(block * 8, 8), pl.ds(top, RC), :].reshape(8 * RC, ROWS)
        return jnp.dot(x, res0[...], preferred_element_type=F32).reshape(8, RC, COLS)

    def write0(c, x):
        prints[2 * brick, c] = x

    march(samples0, coef, write0)
    half = RC // 2
    for r in range(half):
        x = jnp.concatenate([bricks[brick, top + r], bricks[brick, top + r + half]], axis=0)
        y = lax.dot_general(x, res1[...], (((0,), (0,)), ((), ())), preferred_element_type=F32)
        samples[pl.ds(r, 64, stride=RC), :] = y[:, :COLS]
        samples[pl.ds(r + half, 64, stride=RC), :] = y[:, COLS:]

    def samples1(block):
        return samples[pl.ds(block * 8 * RC, 8 * RC), :].reshape(8, RC, COLS)

    def write1(c, x):
        prints[2 * brick + 1, c] = x

    march(samples1, coef, write1)


def depth_table(tag_land, table):
    tags = tag_land[:, 0, :]
    col = jnp.concatenate([tags[:, 0:1], tags[:, 1:2]], axis=0)
    sub = lax.broadcasted_iota(I32, (SLOTS, SLOTS), 0)
    lane = lax.broadcasted_iota(I32, (SLOTS, SLOTS), 1)
    key_col = jnp.broadcast_to(col, (SLOTS, SLOTS)) * SLOTS + sub
    key_row = jnp.broadcast_to(jnp.sum(jnp.where(sub == lane, key_col, 0), axis=0, keepdims=True), (SLOTS, SLOTS))
    place_col = jnp.broadcast_to(
        jnp.sum(jnp.where(key_row < key_col, 1, 0), axis=1, keepdims=True), (SLOTS, SLOTS)
    )
    slot_col = (sub % OWNERS) * 2 + sub // OWNERS
    order = jnp.sum(jnp.where(place_col == lane, slot_col, 0), axis=0, keepdims=True)
    sorted_row = jnp.broadcast_to(
        jnp.sum(jnp.where(place_col == lane, key_col, 0), axis=0, keepdims=True), (SLOTS, SLOTS)
    )
    place_row = jnp.broadcast_to(
        jnp.sum(jnp.where(sub == lane, place_col, 0), axis=0, keepdims=True), (SLOTS, SLOTS)
    )
    sorted_col = jnp.broadcast_to(
        jnp.sum(jnp.where(place_row == sub, key_row, 0), axis=1, keepdims=True), (SLOTS, SLOTS)
    )
    target_row = (sorted_row // SLOTS) % TARGETS
    target_col = (sorted_col // SLOTS) % TARGETS
    mate = (target_row == target_col) & (sub < lane)
    prev = jnp.max(jnp.where(mate, sub, -1), axis=0, keepdims=True)
    prev = jnp.where(prev < 0, SLOTS, prev)
    mine = (target_col == lane) & (sorted_col < EMPTY * SLOTS)
    last = jnp.max(jnp.where(mine, sub, -1), axis=0, keepdims=True)
    last = jnp.where(last < 0, SLOTS, last)
    table[0:1, 0:SLOTS] = order
    table[1:2, 0:SLOTS] = prev
    table[2:3, 0:SLOTS] = last


def kernel(
    item_of, chain, slope, pivot, tag_send, res0, res1, volume,
    colour, light_out,
    bricks, prints, samples, stage, landed, local, run, pieces, bands, band, tag_land, table, table_s,
    vol_sem, send_sem, recv_sem, out_sem, in_sem, tag_out, tag_in, table_sem,
):
    slab = lax.axis_index("depth")
    tile = lax.axis_index("tile")
    z, y = tile // NY, tile % NY

    def hop(j):
        m = j // NY
        return (2 * (m % 2) - 1) * ((m + 1) // 2), j % NY

    def peer(j):
        dz, dy = hop(j)
        return ((z + dz + NZ) % NZ) * NY + (y + dy) % NY

    def source(j):
        dz, dy = hop(j)
        return ((z - dz + NZ) % NZ) * NY + (y - dy + NY) % NY

    def brick_copy(b):
        return pltpu.make_async_copy(volume.at[b], bricks.at[b], vol_sem.at[b])

    def tile_copy(chunk, j, land):
        return pltpu.make_async_remote_copy(
            src_ref=stage.at[chunk, pl.ds(2 * peer(j), 2)],
            dst_ref=landed.at[chunk, pl.ds(2 * land, 2)],
            send_sem=send_sem.at[chunk, j],
            recv_sem=recv_sem.at[chunk, j],
            device_id={"tile": peer(j)},
            device_id_type=MESH,
        )

    def tag_copy(j, land):
        return pltpu.make_async_remote_copy(
            src_ref=tag_send.at[peer(j)],
            dst_ref=tag_land.at[land],
            send_sem=tag_out.at[j],
            recv_sem=tag_in.at[j],
            device_id={"tile": peer(j)},
            device_id_type=MESH,
        )

    def slab_copy(chunk, e, land):
        there = (slab + e) % SLABS
        return pltpu.make_async_remote_copy(
            src_ref=pieces.at[chunk, pl.ds(2 * there, 2)],
            dst_ref=bands.at[chunk, pl.ds(2 * land, 2)],
            send_sem=out_sem.at[chunk, e],
            recv_sem=in_sem.at[chunk, e],
            device_id={"depth": there},
            device_id_type=MESH,
        )

    def each(low, high, do):
        def step(i, _):
            do(i)
            return 0

        lax.fori_loop(low, high, step, 0)

    each(0, BRICKS, lambda b: brick_copy(b).start())
    barrier = pltpu.get_barrier_semaphore()
    each(
        1,
        OWNERS,
        lambda j: pl.semaphore_signal(barrier, inc=1, device_id={"tile": peer(j)}, device_id_type=MESH),
    )
    each(
        1,
        SLABS,
        lambda e: pl.semaphore_signal(
            barrier, inc=1, device_id={"depth": (slab + e) % SLABS}, device_id_type=MESH
        ),
    )
    coef = []
    for c in range(3):
        half = slope[c] * 0.5
        coef.append((half, -half * pivot[c]))
    run[SLOTS] = jnp.zeros((4, RC, COLS), F32)
    table[...] = jnp.zeros_like(table)
    tag_land[tile] = tag_send[tile]
    pl.semaphore_wait(barrier, OWNERS + SLABS - 2)
    each(1, OWNERS, lambda j: tag_copy(j, tile).start())

    def render_and_send(chunk):
        def one(b):
            @pl.when(chunk == 0)
            def _():
                brick_copy(b).wait()

            render_rows(b, chunk, coef, res0, res1, bricks, samples, prints)

        each(0, BRICKS, one)

        def pick(i):
            stage[chunk, i] = prints[item_of[i]]

        each(0, SLOTS, pick)
        each(1, OWNERS, lambda j: tile_copy(chunk, j, tile).start())
        landed[chunk, pl.ds(2 * tile, 2)] = stage[chunk, pl.ds(2 * tile, 2)]

    each(0, CHUNKS, render_and_send)

    each(1, OWNERS, lambda j: tag_copy(j, source(j)).wait())
    depth_table(tag_land, table)
    scalars = pltpu.make_async_copy(table, table_s, table_sem)
    scalars.start()
    scalars.wait()

    def compose_and_send(chunk):
        each(1, OWNERS, lambda j: tile_copy(chunk, j, source(j)).wait())

        def keep(i):
            local[i] = landed[chunk, i]

        each(0, SLOTS, keep)

        def layer(p):
            x = local[table_s[0, p]].astype(F32)
            base = run[table_s[1, p]]
            shade = jnp.exp(-base[3])
            for c in range(3):
                run[p, c] = base[c] + x[c] * shade
            run[p, 3] = base[3] + x[3]

        each(0, SLOTS, layer)

        def close(t):
            pieces[chunk, t] = run[table_s[2, t]].astype(BF)

        each(0, TARGETS, close)
        each(1, SLABS, lambda e: slab_copy(chunk, e, slab).start())
        bands[chunk, pl.ds(2 * slab, 2)] = pieces[chunk, pl.ds(2 * slab, 2)]

    each(0, CHUNKS, compose_and_send)

    def blend(chunk):
        each(1, SLABS, lambda e: slab_copy(chunk, e, (slab - e + SLABS) % SLABS).wait())
        band[...] = bands[chunk]
        rows = pl.ds(pl.multiple_of(chunk * RC, RC), RC)
        for view in range(2):
            front = jnp.zeros((RC, COLS), F32)
            acc = [front] * 3
            for j in range(SLABS):
                x = band[chain[view * SLABS + j] * 2 + view].astype(F32)
                shade = jnp.exp(-front)
                for c in range(3):
                    acc[c] = acc[c] + shade * x[c]
                front = front + x[3]
            for c in range(3):
                colour[view, c, 0, rows, :] = acc[c]
            light_out[view, 0, rows, :] = jnp.exp(-front)

    each(0, CHUNKS, blend)


def body(volume, resampler, slope, pivot, tile_owner, tile_cell, depth_order, slab_rank):
    ids = jnp.arange(ITEMS)
    owner = tile_owner.reshape(-1)
    same = (owner[None, :] == owner[:, None]) & (ids[None, :] < ids[:, None])
    place = owner * 2 + jnp.sum(same.astype(I32), axis=1)
    view = jnp.tile(jnp.arange(2, dtype=I32), BRICKS)
    tag = depth_order.T.reshape(-1) * TARGETS + tile_cell.reshape(-1) * 2 + view
    hit = place[None, :] == jnp.arange(SLOTS, dtype=I32)[:, None]
    item_of = jnp.sum(jnp.where(hit, ids[None, :], 0), axis=1)
    slot_tag = jnp.min(jnp.where(hit, tag[None, :], EMPTY), axis=1).reshape(OWNERS, 1, 2)
    tag_send = jnp.broadcast_to(jnp.pad(slot_tag, ((0, 0), (0, 0), (0, 126))), (OWNERS, 8, 128))
    slabs = jnp.arange(SLABS, dtype=I32)
    chain = jnp.sum(
        jnp.where(slab_rank[:, None, :] == slabs[None, :, None], slabs[None, None, :], 0), axis=2
    ).reshape(-1)
    res0 = resampler[0]
    zero = jnp.zeros_like(res0)
    res1 = jnp.concatenate(
        [jnp.concatenate([resampler[1], zero], 1), jnp.concatenate([zero, resampler[1]], 1)], 0
    )
    smem = pl.BlockSpec(memory_space=pltpu.SMEM)
    vmem = pl.BlockSpec(memory_space=pltpu.VMEM)
    dma = pltpu.SemaphoreType.DMA
    return tuple(
        pl.pallas_call(
            kernel,
            in_specs=[smem, smem, smem, smem, vmem, vmem, vmem, pl.BlockSpec(memory_space=pl.ANY)],
            out_specs=[vmem, vmem],
            out_shape=[
                jax.ShapeDtypeStruct((2, 3, 1, ROWS, COLS), F32),
                jax.ShapeDtypeStruct((2, 1, ROWS, COLS), F32),
            ],
            scratch_shapes=[
                pltpu.VMEM((BRICKS, ROWS, ROWS, ROWS), BF),
                pltpu.VMEM((ITEMS, 4, RC, COLS), BF),
                pltpu.VMEM((64 * RC, COLS), F32),
                pltpu.VMEM((CHUNKS, SLOTS, 4, RC, COLS), BF),
                pltpu.VMEM((CHUNKS, SLOTS, 4, RC, COLS), BF),
                pltpu.VMEM((SLOTS, 4, RC, COLS), BF),
                pltpu.VMEM((SLOTS + 1, 4, RC, COLS), F32),
                pltpu.VMEM((CHUNKS, TARGETS, 4, RC, COLS), BF),
                pltpu.VMEM((CHUNKS, TARGETS, 4, RC, COLS), BF),
                pltpu.VMEM((TARGETS, 4, RC, COLS), BF),
                pltpu.VMEM((OWNERS, 8, 128), I32),
                pltpu.VMEM((8, 128), I32),
                pltpu.SMEM((8, 128), I32),
                dma((BRICKS,)),
                dma((CHUNKS, OWNERS)),
                dma((CHUNKS, OWNERS)),
                dma((CHUNKS, SLABS)),
                dma((CHUNKS, SLABS)),
                dma((OWNERS,)),
                dma((OWNERS,)),
                dma(()),
            ],
            compiler_params=pltpu.CompilerParams(
                collective_id=0, has_side_effects=True, vmem_limit_bytes=52 << 20
            ),
            name="composite",
        )(item_of, chain, slope, pivot, tag_send, res0, res1, volume)
    )


def solution(mesh):
    in_specs = (
        P(("depth", "tile"), None, None, None),
        P(),
        P(),
        P(),
        P(("depth", "tile"), None),
        P(("depth", "tile"), None),
        P(None, ("depth", "tile")),
        P(),
    )
    out_specs = (P(None, None, "tile", "depth", None), P(None, "tile", "depth", None))
    return jax.shard_map(body, mesh=mesh, in_specs=in_specs, out_specs=out_specs, check_vma=False)
```

```python
import jax
import jax.numpy as jnp
from jax import lax
from jax.experimental import pallas as pl
from jax.experimental.pallas import tpu as pltpu
from jax.sharding import PartitionSpec as P

BF = jnp.bfloat16
F32 = jnp.float32
I32 = jnp.int32
MESH = pl.DeviceIdType.MESH
ROWS = 64
COLS = 128
BRICKS = 16
ITEMS = 2 * BRICKS
NZ, NY = 8, 4
OWNERS = NZ * NY
SLABS = 8
SLOTS = 64
TARGETS = 16
RC = 16
CHUNKS = ROWS // RC
EMPTY = 1 << 20
UNROLL = 8
BLOCK = 7 * RC
EXP_SCALE = -1.4426950408889634 / 64.0


SAMPLE_SCRATCH = [pltpu.VMEM((64 * RC, COLS), F32), pltpu.VMEM((64 * RC, COLS), F32)]
HALF = RC // 2


def prepare(brick, chunk, pair, wide, bricks, samples, thick):
    top = pl.multiple_of(chunk * RC, RC)
    x = jnp.concatenate([bricks[brick, top + pair], bricks[brick, top + pair + HALF]], axis=0)
    y = lax.dot_general(x, wide[1], (((0,), (0,)), ((), ())), preferred_element_type=F32)
    samples[pl.ds(pair, 64, stride=RC), :] = y[:, :COLS]
    samples[pl.ds(pair + HALF, 64, stride=RC), :] = y[:, COLS:]
    ones = jnp.ones((8, ROWS), BF)
    total = lax.dot_general(ones, x, (((1,), (1,)), ((), ())), preferred_element_type=F32)
    thick[pl.ds(pair, 1), :] = total[0:1]


def march(brick, chunk, next_brick, next_chunk, coef, res, wide, bricks, prints, sums, now, later):
    samples, other = now
    top = pl.multiple_of(chunk * RC, RC)
    zero = jnp.zeros((RC, COLS), F32)
    start = (zero, zero + 1.0, zero, zero, zero)

    def step(block, carry):
        thick, *views = carry
        cube = bricks[brick, pl.ds(block * 8, 8), pl.ds(top, RC), :]
        x = cube.reshape(8 * RC, ROWS)
        rows = [
            jnp.dot(x, res[0], preferred_element_type=F32).reshape(8, RC, COLS),
            samples[pl.ds(block * 8 * RC, 8 * RC), :].reshape(8, RC, COLS),
        ]
        thick = thick + jnp.sum(cube.astype(F32), axis=0)
        prepare(next_brick, next_chunk, block, wide, bricks, *later)
        for j in range(8):
            for view in range(2):
                front, light, *acc = views[view]
                s = rows[view][j]
                front = front + s
                after = jnp.exp2(front * EXP_SCALE)
                weight = light - after
                for c in range(3):
                    acc[c] = acc[c] + weight * jnp.tanh(s * coef[c][0] + coef[c][1])
                views[view] = (front, after, *acc)
        return (thick, *views)

    thick, *views = lax.fori_loop(
        0, 8, step, (jnp.zeros((RC, ROWS), F32), start, start), unroll=UNROLL
    )
    sums[2 * brick] = jnp.concatenate([thick[:HALF], thick[HALF:]], axis=1)
    sums[2 * brick + 1] = other[...]
    for view in range(2):
        _, light, *acc = views[view]
        for c in range(3):
            prints[2 * brick + view, pl.ds(c * RC, RC), :] = (0.5 * ((1.0 - light) + acc[c])).astype(BF)


def depth_table(tag_land, table):
    tags = tag_land[:, 0, :]
    col = jnp.concatenate([tags[:, 0:1], tags[:, 1:2]], axis=0)
    sub = lax.broadcasted_iota(I32, (SLOTS, SLOTS), 0)
    lane = lax.broadcasted_iota(I32, (SLOTS, SLOTS), 1)
    key_col = jnp.broadcast_to(col, (SLOTS, SLOTS)) * SLOTS + sub
    key_row = jnp.broadcast_to(jnp.sum(jnp.where(sub == lane, key_col, 0), axis=0, keepdims=True), (SLOTS, SLOTS))
    place_col = jnp.broadcast_to(
        jnp.sum(jnp.where(key_row < key_col, 1, 0), axis=1, keepdims=True), (SLOTS, SLOTS)
    )
    slot_col = (sub % OWNERS) * 2 + sub // OWNERS
    order = jnp.sum(jnp.where(place_col == lane, slot_col, 0), axis=0, keepdims=True)
    sorted_row = jnp.broadcast_to(
        jnp.sum(jnp.where(place_col == lane, key_col, 0), axis=0, keepdims=True), (SLOTS, SLOTS)
    )
    place_row = jnp.broadcast_to(
        jnp.sum(jnp.where(sub == lane, place_col, 0), axis=0, keepdims=True), (SLOTS, SLOTS)
    )
    sorted_col = jnp.broadcast_to(
        jnp.sum(jnp.where(place_row == sub, key_row, 0), axis=1, keepdims=True), (SLOTS, SLOTS)
    )
    target_row = (sorted_row // SLOTS) % TARGETS
    target_col = (sorted_col // SLOTS) % TARGETS
    mate = (target_row == target_col) & (sub < lane)
    prev = jnp.max(jnp.where(mate, sub, -1), axis=0, keepdims=True)
    prev = jnp.where(prev < 0, SLOTS, prev)
    mine = (target_col == lane) & (sorted_col < EMPTY * SLOTS)
    last = jnp.max(jnp.where(mine, sub, -1), axis=0, keepdims=True)
    last = jnp.where(last < 0, SLOTS, last)
    table[0:1, 0:SLOTS] = order
    table[1:2, 0:SLOTS] = prev
    table[2:3, 0:SLOTS] = last
    table[3:4, 0:SLOTS] = (sorted_row[0:1] // SLOTS) % 2


def kernel(
    item_of, chain, slope, pivot, tag_send, res, volume,
    colour, light_out,
    wide, bricks, prints, sums, samples_a, samples_b, thick_a, thick_b, stage, landed, local, depths, run, pieces, bands, band, tag_land, table, table_s,
    vol_sem, send_sem, recv_sem, out_sem, in_sem, tag_out, tag_in, table_sem,
):
    slab = lax.axis_index("depth")
    tile = lax.axis_index("tile")
    z, y = tile // NY, tile % NY

    def hop(j):
        m = j // NY
        return (2 * (m % 2) - 1) * ((m + 1) // 2), j % NY

    def peer(j):
        dz, dy = hop(j)
        return ((z + dz + NZ) % NZ) * NY + (y + dy) % NY

    def source(j):
        dz, dy = hop(j)
        return ((z - dz + NZ) % NZ) * NY + (y - dy + NY) % NY

    def brick_copy(b):
        return pltpu.make_async_copy(volume.at[b], bricks.at[b], vol_sem.at[b])

    def tile_copy(chunk, j, land):
        return pltpu.make_async_remote_copy(
            src_ref=stage.at[chunk, peer(j)],
            dst_ref=landed.at[chunk, land],
            send_sem=send_sem.at[chunk, j],
            recv_sem=recv_sem.at[chunk, j],
            device_id={"tile": peer(j)},
            device_id_type=MESH,
        )

    def tag_copy(j, land):
        return pltpu.make_async_remote_copy(
            src_ref=tag_send.at[peer(j)],
            dst_ref=tag_land.at[land],
            send_sem=tag_out.at[j],
            recv_sem=tag_in.at[j],
            device_id={"tile": peer(j)},
            device_id_type=MESH,
        )

    def slab_copy(chunk, e, land):
        there = (slab + e) % SLABS
        return pltpu.make_async_remote_copy(
            src_ref=pieces.at[chunk, pl.ds(2 * there, 2)],
            dst_ref=bands.at[chunk, pl.ds(2 * land, 2)],
            send_sem=out_sem.at[chunk, e],
            recv_sem=in_sem.at[chunk, e],
            device_id={"depth": there},
            device_id_type=MESH,
        )

    def each(low, high, do):
        def step(i, _):
            do(i)
            return 0

        lax.fori_loop(low, high, step, 0)

    each(0, BRICKS, lambda b: brick_copy(b).start())
    barrier = pltpu.get_barrier_semaphore()
    each(
        1,
        OWNERS,
        lambda j: pl.semaphore_signal(barrier, inc=1, device_id={"tile": peer(j)}, device_id_type=MESH),
    )
    each(
        1,
        SLABS,
        lambda e: pl.semaphore_signal(
            barrier, inc=1, device_id={"depth": (slab + e) % SLABS}, device_id_type=MESH
        ),
    )
    coef = []
    for c in range(3):
        half = slope[c] * 0.5
        coef.append((half, -half * pivot[c]))
    wide[...] = jnp.zeros_like(wide)
    for view in range(2):
        wide[view, 0:ROWS, 0:COLS] = res[view]
        wide[view, ROWS : 2 * ROWS, COLS : 2 * COLS] = res[view]
    run[SLOTS] = jnp.zeros((4, RC, COLS), F32)
    table[...] = jnp.zeros_like(table)
    tag_land[tile] = tag_send[tile]
    pl.semaphore_wait(barrier, OWNERS + SLABS - 2)
    each(1, OWNERS, lambda j: tag_copy(j, tile).start())

    even, odd = (samples_a, thick_a), (samples_b, thick_b)
    brick_copy(0).wait()
    each(0, HALF, lambda pair: prepare(0, 0, pair, wide, bricks, *even))

    def render_and_send(chunk):
        def one(b):
            shared = (coef, res, wide, bricks, prints, sums)
            first, second = 2 * b, 2 * b + 1

            @pl.when(chunk == 0)
            def _():
                brick_copy(second).wait()

            march(first, chunk, second, chunk, *shared, even, odd)
            wrap = second // (BRICKS - 1)

            @pl.when((chunk == 0) & (b < BRICKS // 2 - 1))
            def _():
                brick_copy(second + 1).wait()

            march(
                second, chunk, (second + 1) % BRICKS, (chunk + wrap) % CHUNKS, *shared, odd, even
            )

        each(0, BRICKS // 2, one)

        def pick(o):
            one, two = item_of[2 * o], item_of[2 * o + 1]
            stage[chunk, o, 0 : 3 * RC, :] = prints[one]
            stage[chunk, o, 3 * RC : 6 * RC, :] = prints[two]
            stage[chunk, o, 6 * RC : BLOCK, :] = jnp.concatenate([sums[one], sums[two]], axis=0).astype(BF)

        each(0, OWNERS, pick)
        each(1, OWNERS, lambda j: tile_copy(chunk, j, tile).start())
        landed[chunk, tile] = stage[chunk, tile]

    each(0, CHUNKS, render_and_send)

    each(1, OWNERS, lambda j: tag_copy(j, source(j)).wait())
    depth_table(tag_land, table)
    scalars = pltpu.make_async_copy(table, table_s, table_sem)
    scalars.start()
    scalars.wait()

    def compose_and_send(chunk):
        each(1, OWNERS, lambda j: tile_copy(chunk, j, source(j)).wait())

        def keep(g):
            for i in range(8):
                src = g * 8 + i
                local[2 * src] = landed[chunk, src, 0 : 3 * RC, :]
                local[2 * src + 1] = landed[chunk, src, 3 * RC : 6 * RC, :]
            x = landed[chunk, pl.ds(g * 8, 8), 6 * RC : BLOCK, :].reshape(8 * RC, 2 * ROWS)
            for view in range(2):
                d = jnp.dot(x, wide[view], preferred_element_type=F32)
                depths[view, pl.ds(16 * g, 16)] = (d * (1.0 / 64.0)).reshape(16, HALF, 2 * COLS)

        each(0, OWNERS // 8, keep)

        def layer(p):
            slot = table_s[0, p]
            x = local[slot].astype(F32)
            d = depths[table_s[3, p], slot]
            base = run[table_s[1, p]]
            shade = jnp.exp(-base[3])
            run[p, 3] = base[3] + jnp.concatenate([d[:, :COLS], d[:, COLS:]], axis=0)
            for c in range(3):
                run[p, c] = base[c] + x[c * RC : (c + 1) * RC] * shade

        each(0, SLOTS, layer)

        def close(t):
            pieces[chunk, t] = run[table_s[2, t]].astype(BF)

        each(0, TARGETS, close)
        each(1, SLABS, lambda e: slab_copy(chunk, e, slab).start())
        bands[chunk, pl.ds(2 * slab, 2)] = pieces[chunk, pl.ds(2 * slab, 2)]

    each(0, CHUNKS, compose_and_send)

    def blend(chunk):
        each(1, SLABS, lambda e: slab_copy(chunk, e, (slab - e + SLABS) % SLABS).wait())
        band[...] = bands[chunk]
        rows = pl.ds(pl.multiple_of(chunk * RC, RC), RC)
        for view in range(2):
            front = jnp.zeros((RC, COLS), F32)
            acc = [front] * 3
            for j in range(SLABS):
                x = band[chain[view * SLABS + j] * 2 + view].astype(F32)
                shade = jnp.exp(-front)
                for c in range(3):
                    acc[c] = acc[c] + shade * x[c]
                front = front + x[3]
            for c in range(3):
                colour[view, c, 0, rows, :] = acc[c]
            light_out[view, 0, rows, :] = jnp.exp(-front)

    each(0, CHUNKS, blend)


def body(volume, resampler, slope, pivot, tile_owner, tile_cell, depth_order, slab_rank):
    ids = jnp.arange(ITEMS)
    owner = tile_owner.reshape(-1)
    same = (owner[None, :] == owner[:, None]) & (ids[None, :] < ids[:, None])
    place = owner * 2 + jnp.sum(same.astype(I32), axis=1)
    view = jnp.tile(jnp.arange(2, dtype=I32), BRICKS)
    tag = depth_order.T.reshape(-1) * TARGETS + tile_cell.reshape(-1) * 2 + view
    hit = place[None, :] == jnp.arange(SLOTS, dtype=I32)[:, None]
    item_of = jnp.sum(jnp.where(hit, ids[None, :], 0), axis=1)
    slot_tag = jnp.min(jnp.where(hit, tag[None, :], EMPTY), axis=1).reshape(OWNERS, 1, 2)
    tag_send = jnp.broadcast_to(jnp.pad(slot_tag, ((0, 0), (0, 0), (0, 126))), (OWNERS, 8, 128))
    slabs = jnp.arange(SLABS, dtype=I32)
    chain = jnp.sum(
        jnp.where(slab_rank[:, None, :] == slabs[None, :, None], slabs[None, None, :], 0), axis=2
    ).reshape(-1)
    smem = pl.BlockSpec(memory_space=pltpu.SMEM)
    vmem = pl.BlockSpec(memory_space=pltpu.VMEM)
    dma = pltpu.SemaphoreType.DMA
    return tuple(
        pl.pallas_call(
            kernel,
            in_specs=[smem, smem, smem, smem, vmem, vmem, pl.BlockSpec(memory_space=pl.ANY)],
            out_specs=[vmem, vmem],
            out_shape=[
                jax.ShapeDtypeStruct((2, 3, 1, ROWS, COLS), F32),
                jax.ShapeDtypeStruct((2, 1, ROWS, COLS), F32),
            ],
            scratch_shapes=[
                pltpu.VMEM((2, 2 * ROWS, 2 * COLS), BF),
                pltpu.VMEM((BRICKS, ROWS, ROWS, ROWS), BF),
                pltpu.VMEM((ITEMS, 3 * RC, COLS), BF),
                pltpu.VMEM((ITEMS, HALF, 2 * ROWS), F32),
                *SAMPLE_SCRATCH,
                pltpu.VMEM((HALF, 2 * ROWS), F32),
                pltpu.VMEM((HALF, 2 * ROWS), F32),
                pltpu.VMEM((CHUNKS, OWNERS, BLOCK, COLS), BF),
                pltpu.VMEM((CHUNKS, OWNERS, BLOCK, COLS), BF),
                pltpu.VMEM((SLOTS, 3 * RC, COLS), BF),
                pltpu.VMEM((2, SLOTS, HALF, 2 * COLS), F32),
                pltpu.VMEM((SLOTS + 1, 4, RC, COLS), F32),
                pltpu.VMEM((CHUNKS, TARGETS, 4, RC, COLS), BF),
                pltpu.VMEM((CHUNKS, TARGETS, 4, RC, COLS), BF),
                pltpu.VMEM((TARGETS, 4, RC, COLS), BF),
                pltpu.VMEM((OWNERS, 8, 128), I32),
                pltpu.VMEM((8, 128), I32),
                pltpu.SMEM((8, 128), I32),
                dma((BRICKS,)),
                dma((CHUNKS, OWNERS)),
                dma((CHUNKS, OWNERS)),
                dma((CHUNKS, SLABS)),
                dma((CHUNKS, SLABS)),
                dma((OWNERS,)),
                dma((OWNERS,)),
                dma(()),
            ],
            compiler_params=pltpu.CompilerParams(
                collective_id=0, has_side_effects=True, vmem_limit_bytes=52 << 20
            ),
            name="composite",
        )(item_of, chain, slope, pivot, tag_send, resampler, volume)
    )


def solution(mesh):
    in_specs = (
        P(("depth", "tile"), None, None, None),
        P(),
        P(),
        P(),
        P(("depth", "tile"), None),
        P(("depth", "tile"), None),
        P(None, ("depth", "tile")),
        P(),
    )
    out_specs = (P(None, None, "tile", "depth", None), P(None, "tile", "depth", None))
    return jax.shard_map(body, mesh=mesh, in_specs=in_specs, out_specs=out_specs, check_vma=False)
```

```python
import jax
import jax.numpy as jnp
from jax import lax
from jax.experimental import pallas as pl
from jax.experimental.pallas import tpu as pltpu
from jax.sharding import PartitionSpec as P

BF = jnp.bfloat16
F32 = jnp.float32
I32 = jnp.int32
MESH = pl.DeviceIdType.MESH
ROWS = 64
COLS = 128
BRICKS = 16
ITEMS = 2 * BRICKS
NZ, NY = 8, 4
OWNERS = NZ * NY
SLABS = 8
SLOTS = 64
TARGETS = 16
RC = 16
CHUNKS = ROWS // RC
EMPTY = 1 << 20
UNROLL = 8
BLOCK = 7 * RC
EXP_SCALE = -1.4426950408889634 / 64.0


SAMPLE_SCRATCH = [pltpu.VMEM((64 * RC, COLS), F32), pltpu.VMEM((64 * RC, COLS), F32)]
HALF = RC // 2


def prepare(brick, chunk, pair, wide, bricks, samples, thick):
    top = pl.multiple_of(chunk * RC, RC)
    x = jnp.concatenate([bricks[brick, top + pair], bricks[brick, top + pair + HALF]], axis=0)
    y = lax.dot_general(x, wide[1], (((0,), (0,)), ((), ())), preferred_element_type=F32)
    samples[pl.ds(pair, 64, stride=RC), :] = y[:, :COLS]
    samples[pl.ds(pair + HALF, 64, stride=RC), :] = y[:, COLS:]
    ones = jnp.ones((8, ROWS), BF)
    total = lax.dot_general(ones, x, (((1,), (1,)), ((), ())), preferred_element_type=F32)
    thick[pl.ds(pair, 1), :] = total[0:1]


def march(brick, chunk, next_brick, next_chunk, coef, res, wide, bricks, prints, sums, now, later):
    samples, other = now
    top = pl.multiple_of(chunk * RC, RC)
    zero = jnp.zeros((RC, COLS), F32)
    start = (zero, zero + 1.0, zero, zero, zero)

    def step(block, carry):
        thick, *views = carry
        cube = bricks[brick, pl.ds(block * 8, 8), pl.ds(top, RC), :]
        x = cube.reshape(8 * RC, ROWS)
        rows = [
            jnp.dot(x, res[0], preferred_element_type=F32).reshape(8, RC, COLS),
            samples[pl.ds(block * 8 * RC, 8 * RC), :].reshape(8, RC, COLS),
        ]
        thick = thick + jnp.sum(cube.astype(F32), axis=0)
        prepare(next_brick, next_chunk, block, wide, bricks, *later)
        for j in range(8):
            for view in range(2):
                front, light, *acc = views[view]
                s = rows[view][j]
                front = front + s
                after = jnp.exp2(front * EXP_SCALE)
                weight = light - after
                for c in range(3):
                    acc[c] = acc[c] + weight * jnp.tanh(s * coef[c][0] + coef[c][1])
                views[view] = (front, after, *acc)
        return (thick, *views)

    thick, *views = lax.fori_loop(
        0, 8, step, (jnp.zeros((RC, ROWS), F32), start, start), unroll=UNROLL
    )
    sums[2 * brick] = jnp.concatenate([thick[:HALF], thick[HALF:]], axis=1)
    sums[2 * brick + 1] = other[...]
    for view in range(2):
        _, light, *acc = views[view]
        for c in range(3):
            prints[2 * brick + view, pl.ds(c * RC, RC), :] = (0.5 * ((1.0 - light) + acc[c])).astype(BF)


def depth_table(tag_land, table):
    tags = tag_land[:, 0, :]
    col = jnp.concatenate([tags[:, 0:1], tags[:, 1:2]], axis=0)
    sub = lax.broadcasted_iota(I32, (SLOTS, SLOTS), 0)
    lane = lax.broadcasted_iota(I32, (SLOTS, SLOTS), 1)
    key_col = jnp.broadcast_to(col, (SLOTS, SLOTS)) * SLOTS + sub
    key_row = jnp.broadcast_to(jnp.sum(jnp.where(sub == lane, key_col, 0), axis=0, keepdims=True), (SLOTS, SLOTS))
    place_col = jnp.broadcast_to(
        jnp.sum(jnp.where(key_row < key_col, 1, 0), axis=1, keepdims=True), (SLOTS, SLOTS)
    )
    slot_col = (sub % OWNERS) * 2 + sub // OWNERS
    order = jnp.sum(jnp.where(place_col == lane, slot_col, 0), axis=0, keepdims=True)
    sorted_row = jnp.broadcast_to(
        jnp.sum(jnp.where(place_col == lane, key_col, 0), axis=0, keepdims=True), (SLOTS, SLOTS)
    )
    place_row = jnp.broadcast_to(
        jnp.sum(jnp.where(sub == lane, place_col, 0), axis=0, keepdims=True), (SLOTS, SLOTS)
    )
    sorted_col = jnp.broadcast_to(
        jnp.sum(jnp.where(place_row == sub, key_row, 0), axis=1, keepdims=True), (SLOTS, SLOTS)
    )
    target_row = (sorted_row // SLOTS) % TARGETS
    target_col = (sorted_col // SLOTS) % TARGETS
    mate = (target_row == target_col) & (sub < lane)
    prev = jnp.max(jnp.where(mate, sub, -1), axis=0, keepdims=True)
    prev = jnp.where(prev < 0, SLOTS, prev)
    mine = (target_col == lane) & (sorted_col < EMPTY * SLOTS)
    last = jnp.max(jnp.where(mine, sub, -1), axis=0, keepdims=True)
    last = jnp.where(last < 0, SLOTS, last)
    table[0:1, 0:SLOTS] = order
    table[1:2, 0:SLOTS] = prev
    table[2:3, 0:SLOTS] = last
    table[3:4, 0:SLOTS] = (sorted_row[0:1] // SLOTS) % 2


def kernel(
    item_of, chain, slope, pivot, tag_send, res, volume,
    colour, light_out,
    wide, bricks, prints, sums, samples_a, samples_b, thick_a, thick_b, stage, landed, local, depths, run, pieces, bands, band, tag_land, table, table_s,
    vol_sem, send_sem, recv_sem, out_sem, in_sem, tag_out, tag_in, table_sem,
):
    slab = lax.axis_index("depth")
    tile = lax.axis_index("tile")
    z, y = tile // NY, tile % NY

    planes = [(z + dz) % NZ for dz in range(NZ)]
    columns = [(y + dy) % NY for dy in range(NY)]

    def hop(j):
        m = j // NY
        return (2 * (m % 2) - 1) * ((m + 1) // 2), j % NY

    def peer(j):
        dz, dy = hop(j)
        return planes[dz % NZ] * NY + columns[dy]

    def source(j):
        dz, dy = hop(j)
        return planes[-dz % NZ] * NY + columns[-dy % NY]

    def brick_copy(b):
        return pltpu.make_async_copy(volume.at[b], bricks.at[b], vol_sem.at[b])

    def tile_copy(chunk, j, land):
        return pltpu.make_async_remote_copy(
            src_ref=stage.at[chunk, peer(j)],
            dst_ref=landed.at[chunk, land],
            send_sem=send_sem.at[chunk, j],
            recv_sem=recv_sem.at[chunk, j],
            device_id={"tile": peer(j)},
            device_id_type=MESH,
        )

    def tag_copy(j, land):
        return pltpu.make_async_remote_copy(
            src_ref=tag_send.at[peer(j)],
            dst_ref=tag_land.at[land],
            send_sem=tag_out.at[j],
            recv_sem=tag_in.at[j],
            device_id={"tile": peer(j)},
            device_id_type=MESH,
        )

    def slab_copy(chunk, e, land):
        there = (slab + e) % SLABS
        return pltpu.make_async_remote_copy(
            src_ref=pieces.at[chunk, pl.ds(2 * there, 2)],
            dst_ref=bands.at[chunk, pl.ds(2 * land, 2)],
            send_sem=out_sem.at[chunk, e],
            recv_sem=in_sem.at[chunk, e],
            device_id={"depth": there},
            device_id_type=MESH,
        )

    def each(low, high, do):
        def step(i, _):
            do(i)
            return 0

        lax.fori_loop(low, high, step, 0)

    def every(do):
        for j in range(1, OWNERS):
            do(j)

    each(0, BRICKS, lambda b: brick_copy(b).start())
    barrier = pltpu.get_barrier_semaphore()
    every(
        lambda j: pl.semaphore_signal(barrier, inc=1, device_id={"tile": peer(j)}, device_id_type=MESH),
    )
    each(
        1,
        SLABS,
        lambda e: pl.semaphore_signal(
            barrier, inc=1, device_id={"depth": (slab + e) % SLABS}, device_id_type=MESH
        ),
    )
    coef = []
    for c in range(3):
        half = slope[c] * 0.5
        coef.append((half, -half * pivot[c]))
    wide[...] = jnp.zeros_like(wide)
    for view in range(2):
        wide[view, 0:ROWS, 0:COLS] = res[view]
        wide[view, ROWS : 2 * ROWS, COLS : 2 * COLS] = res[view]
    run[SLOTS] = jnp.zeros((4, RC, COLS), F32)
    table[...] = jnp.zeros_like(table)
    tag_land[tile] = tag_send[tile]
    pl.semaphore_wait(barrier, OWNERS + SLABS - 2)
    every(lambda j: tag_copy(j, tile).start())

    even, odd = (samples_a, thick_a), (samples_b, thick_b)
    brick_copy(0).wait()
    each(0, HALF, lambda pair: prepare(0, 0, pair, wide, bricks, *even))

    def render_and_send(chunk):
        def one(b):
            shared = (coef, res, wide, bricks, prints, sums)
            first, second = 2 * b, 2 * b + 1

            @pl.when(chunk == 0)
            def _():
                brick_copy(second).wait()

            march(first, chunk, second, chunk, *shared, even, odd)
            wrap = second // (BRICKS - 1)

            @pl.when((chunk == 0) & (b < BRICKS // 2 - 1))
            def _():
                brick_copy(second + 1).wait()

            march(
                second, chunk, (second + 1) % BRICKS, (chunk + wrap) % CHUNKS, *shared, odd, even
            )

        each(0, BRICKS // 2, one)

        def pick(o):
            one, two = item_of[2 * o], item_of[2 * o + 1]
            stage[chunk, o, 0 : 3 * RC, :] = prints[one]
            stage[chunk, o, 3 * RC : 6 * RC, :] = prints[two]
            stage[chunk, o, 6 * RC : BLOCK, :] = jnp.concatenate([sums[one], sums[two]], axis=0).astype(BF)

        each(0, OWNERS, pick)
        every(lambda j: tile_copy(chunk, j, tile).start())
        landed[chunk, tile] = stage[chunk, tile]

    each(0, CHUNKS, render_and_send)

    every(lambda j: tag_copy(j, source(j)).wait())
    depth_table(tag_land, table)
    scalars = pltpu.make_async_copy(table, table_s, table_sem)
    scalars.start()
    scalars.wait()

    def compose_and_send(chunk):
        every(lambda j: tile_copy(chunk, j, source(j)).wait())

        def keep(g):
            for i in range(8):
                src = g * 8 + i
                local[2 * src] = landed[chunk, src, 0 : 3 * RC, :]
                local[2 * src + 1] = landed[chunk, src, 3 * RC : 6 * RC, :]
            x = landed[chunk, pl.ds(g * 8, 8), 6 * RC : BLOCK, :].reshape(8 * RC, 2 * ROWS)
            for view in range(2):
                d = jnp.dot(x, wide[view], preferred_element_type=F32)
                depths[view, pl.ds(16 * g, 16)] = (d * (1.0 / 64.0)).reshape(16, HALF, 2 * COLS)

        each(0, OWNERS // 8, keep)

        def layer(p):
            slot = table_s[0, p]
            x = local[slot].astype(F32)
            d = depths[table_s[3, p], slot]
            base = run[table_s[1, p]]
            shade = jnp.exp(-base[3])
            run[p, 3] = base[3] + jnp.concatenate([d[:, :COLS], d[:, COLS:]], axis=0)
            for c in range(3):
                run[p, c] = base[c] + x[c * RC : (c + 1) * RC] * shade

        each(0, SLOTS, layer)

        def close(t):
            pieces[chunk, t] = run[table_s[2, t]].astype(BF)

        each(0, TARGETS, close)
        each(1, SLABS, lambda e: slab_copy(chunk, e, slab).start())
        bands[chunk, pl.ds(2 * slab, 2)] = pieces[chunk, pl.ds(2 * slab, 2)]

    each(0, CHUNKS, compose_and_send)

    def blend(chunk):
        each(1, SLABS, lambda e: slab_copy(chunk, e, (slab - e + SLABS) % SLABS).wait())
        band[...] = bands[chunk]
        rows = pl.ds(pl.multiple_of(chunk * RC, RC), RC)
        for view in range(2):
            front = jnp.zeros((RC, COLS), F32)
            acc = [front] * 3
            for j in range(SLABS):
                x = band[chain[view * SLABS + j] * 2 + view].astype(F32)
                shade = jnp.exp(-front)
                for c in range(3):
                    acc[c] = acc[c] + shade * x[c]
                front = front + x[3]
            for c in range(3):
                colour[view, c, 0, rows, :] = acc[c]
            light_out[view, 0, rows, :] = jnp.exp(-front)

    each(0, CHUNKS, blend)


def body(volume, resampler, slope, pivot, tile_owner, tile_cell, depth_order, slab_rank):
    ids = jnp.arange(ITEMS)
    owner = tile_owner.reshape(-1)
    same = (owner[None, :] == owner[:, None]) & (ids[None, :] < ids[:, None])
    place = owner * 2 + jnp.sum(same.astype(I32), axis=1)
    view = jnp.tile(jnp.arange(2, dtype=I32), BRICKS)
    tag = depth_order.T.reshape(-1) * TARGETS + tile_cell.reshape(-1) * 2 + view
    hit = place[None, :] == jnp.arange(SLOTS, dtype=I32)[:, None]
    item_of = jnp.sum(jnp.where(hit, ids[None, :], 0), axis=1)
    slot_tag = jnp.min(jnp.where(hit, tag[None, :], EMPTY), axis=1).reshape(OWNERS, 1, 2)
    tag_send = jnp.broadcast_to(jnp.pad(slot_tag, ((0, 0), (0, 0), (0, 126))), (OWNERS, 8, 128))
    slabs = jnp.arange(SLABS, dtype=I32)
    chain = jnp.sum(
        jnp.where(slab_rank[:, None, :] == slabs[None, :, None], slabs[None, None, :], 0), axis=2
    ).reshape(-1)
    smem = pl.BlockSpec(memory_space=pltpu.SMEM)
    vmem = pl.BlockSpec(memory_space=pltpu.VMEM)
    dma = pltpu.SemaphoreType.DMA
    return tuple(
        pl.pallas_call(
            kernel,
            in_specs=[smem, smem, smem, smem, vmem, vmem, pl.BlockSpec(memory_space=pl.ANY)],
            out_specs=[vmem, vmem],
            out_shape=[
                jax.ShapeDtypeStruct((2, 3, 1, ROWS, COLS), F32),
                jax.ShapeDtypeStruct((2, 1, ROWS, COLS), F32),
            ],
            scratch_shapes=[
                pltpu.VMEM((2, 2 * ROWS, 2 * COLS), BF),
                pltpu.VMEM((BRICKS, ROWS, ROWS, ROWS), BF),
                pltpu.VMEM((ITEMS, 3 * RC, COLS), BF),
                pltpu.VMEM((ITEMS, HALF, 2 * ROWS), F32),
                *SAMPLE_SCRATCH,
                pltpu.VMEM((HALF, 2 * ROWS), F32),
                pltpu.VMEM((HALF, 2 * ROWS), F32),
                pltpu.VMEM((CHUNKS, OWNERS, BLOCK, COLS), BF),
                pltpu.VMEM((CHUNKS, OWNERS, BLOCK, COLS), BF),
                pltpu.VMEM((SLOTS, 3 * RC, COLS), BF),
                pltpu.VMEM((2, SLOTS, HALF, 2 * COLS), F32),
                pltpu.VMEM((SLOTS + 1, 4, RC, COLS), F32),
                pltpu.VMEM((CHUNKS, TARGETS, 4, RC, COLS), BF),
                pltpu.VMEM((CHUNKS, TARGETS, 4, RC, COLS), BF),
                pltpu.VMEM((TARGETS, 4, RC, COLS), BF),
                pltpu.VMEM((OWNERS, 8, 128), I32),
                pltpu.VMEM((8, 128), I32),
                pltpu.SMEM((8, 128), I32),
                dma((BRICKS,)),
                dma((CHUNKS, OWNERS)),
                dma((CHUNKS, OWNERS)),
                dma((CHUNKS, SLABS)),
                dma((CHUNKS, SLABS)),
                dma((OWNERS,)),
                dma((OWNERS,)),
                dma(()),
            ],
            compiler_params=pltpu.CompilerParams(
                collective_id=0, has_side_effects=True, vmem_limit_bytes=52 << 20
            ),
            name="composite",
        )(item_of, chain, slope, pivot, tag_send, resampler, volume)
    )


def solution(mesh):
    in_specs = (
        P(("depth", "tile"), None, None, None),
        P(),
        P(),
        P(),
        P(("depth", "tile"), None),
        P(("depth", "tile"), None),
        P(None, ("depth", "tile")),
        P(),
    )
    out_specs = (P(None, None, "tile", "depth", None), P(None, "tile", "depth", None))
    return jax.shard_map(body, mesh=mesh, in_specs=in_specs, out_specs=out_specs, check_vma=False)
```

```python
import jax
import jax.numpy as jnp
from jax import lax
from jax.experimental import pallas as pl
from jax.experimental.pallas import tpu as pltpu
from jax.sharding import PartitionSpec as P

BF = jnp.bfloat16
F32 = jnp.float32
I32 = jnp.int32
MESH = pl.DeviceIdType.MESH
ROWS = 64
COLS = 128
BRICKS = 16
ITEMS = 2 * BRICKS
NZ, NY = 8, 4
OWNERS = NZ * NY
SLABS = 8
SLOTS = 64
TARGETS = 16
RC = 16
CHUNKS = ROWS // RC
EMPTY = 1 << 20
UNROLL = 8
BLOCK = 7 * RC
EXP_SCALE = -1.4426950408889634 / 64.0


SAMPLE_SCRATCH = [pltpu.VMEM((64 * RC, COLS), F32), pltpu.VMEM((64 * RC, COLS), F32)]
HALF = RC // 2


def prepare(brick, chunk, pair, wide, bricks, samples, thick):
    top = pl.multiple_of(chunk * RC, RC)
    x = jnp.concatenate([bricks[brick, top + pair], bricks[brick, top + pair + HALF]], axis=0)
    y = lax.dot_general(x, wide[1], (((0,), (0,)), ((), ())), preferred_element_type=F32)
    samples[pl.ds(pair, 64, stride=RC), :] = y[:, :COLS]
    samples[pl.ds(pair + HALF, 64, stride=RC), :] = y[:, COLS:]
    ones = jnp.ones((8, ROWS), BF)
    total = lax.dot_general(ones, x, (((1,), (1,)), ((), ())), preferred_element_type=F32)
    thick[pl.ds(pair, 1), :] = total[0:1]


def march(brick, chunk, next_brick, next_chunk, coef, res, wide, bricks, prints, sums, now, later):
    samples, other = now
    top = pl.multiple_of(chunk * RC, RC)
    zero = jnp.zeros((RC, COLS), F32)
    start = (zero, zero + 1.0, zero, zero, zero)

    def step(block, carry):
        thick, *views = carry
        cube = bricks[brick, pl.ds(block * 8, 8), pl.ds(top, RC), :]
        x = cube.reshape(8 * RC, ROWS)
        rows = [
            jnp.dot(x, res[0], preferred_element_type=F32).reshape(8, RC, COLS),
            samples[pl.ds(block * 8 * RC, 8 * RC), :].reshape(8, RC, COLS),
        ]
        thick = thick + jnp.sum(cube.astype(F32), axis=0)
        prepare(next_brick, next_chunk, block, wide, bricks, *later)
        for j in range(8):
            for view in range(2):
                front, light, *acc = views[view]
                s = rows[view][j]
                front = front + s
                after = jnp.exp2(front * EXP_SCALE)
                weight = light - after
                for c in range(3):
                    acc[c] = acc[c] + weight * jnp.tanh(s * coef[c][0] + coef[c][1])
                views[view] = (front, after, *acc)
        return (thick, *views)

    thick, *views = lax.fori_loop(
        0, 8, step, (jnp.zeros((RC, ROWS), F32), start, start), unroll=UNROLL
    )
    sums[2 * brick] = jnp.concatenate([thick[:HALF], thick[HALF:]], axis=1)
    sums[2 * brick + 1] = other[...]
    for view in range(2):
        _, light, *acc = views[view]
        for c in range(3):
            prints[2 * brick + view, pl.ds(c * RC, RC), :] = (0.5 * ((1.0 - light) + acc[c])).astype(BF)


def depth_table(tag_land, table):
    tags = tag_land[:, 0, :]
    col = jnp.concatenate([tags[:, 0:1], tags[:, 1:2]], axis=0)
    sub = lax.broadcasted_iota(I32, (SLOTS, SLOTS), 0)
    lane = lax.broadcasted_iota(I32, (SLOTS, SLOTS), 1)
    key_col = jnp.broadcast_to(col, (SLOTS, SLOTS)) * SLOTS + sub
    key_row = jnp.broadcast_to(jnp.sum(jnp.where(sub == lane, key_col, 0), axis=0, keepdims=True), (SLOTS, SLOTS))
    place_col = jnp.broadcast_to(
        jnp.sum(jnp.where(key_row < key_col, 1, 0), axis=1, keepdims=True), (SLOTS, SLOTS)
    )
    slot_col = (sub % OWNERS) * 2 + sub // OWNERS
    order = jnp.sum(jnp.where(place_col == lane, slot_col, 0), axis=0, keepdims=True)
    sorted_row = jnp.broadcast_to(
        jnp.sum(jnp.where(place_col == lane, key_col, 0), axis=0, keepdims=True), (SLOTS, SLOTS)
    )
    place_row = jnp.broadcast_to(
        jnp.sum(jnp.where(sub == lane, place_col, 0), axis=0, keepdims=True), (SLOTS, SLOTS)
    )
    sorted_col = jnp.broadcast_to(
        jnp.sum(jnp.where(place_row == sub, key_row, 0), axis=1, keepdims=True), (SLOTS, SLOTS)
    )
    target_row = (sorted_row // SLOTS) % TARGETS
    target_col = (sorted_col // SLOTS) % TARGETS
    mate = (target_row == target_col) & (sub < lane)
    prev = jnp.max(jnp.where(mate, sub, -1), axis=0, keepdims=True)
    prev = jnp.where(prev < 0, SLOTS, prev)
    mine = (target_col == lane) & (sorted_col < EMPTY * SLOTS)
    last = jnp.max(jnp.where(mine, sub, -1), axis=0, keepdims=True)
    last = jnp.where(last < 0, SLOTS, last)
    table[0:1, 0:SLOTS] = order
    table[1:2, 0:SLOTS] = prev
    table[2:3, 0:SLOTS] = last
    table[3:4, 0:SLOTS] = (sorted_row[0:1] // SLOTS) % 2


def kernel(
    item_of, chain, slope, pivot, tag_send, res, volume,
    colour, light_out,
    wide, bricks, prints, sums, samples_a, samples_b, thick_a, thick_b, stage, landed, local, depths, run, pieces, bands, band, tag_land, table, table_s,
    vol_sem, send_sem, recv_sem, out_sem, in_sem, tag_out, tag_in, table_sem,
):
    slab = lax.axis_index("depth")
    tile = lax.axis_index("tile")
    z, y = tile // NY, tile % NY

    planes = [(z + dz) % NZ for dz in range(NZ)]
    columns = [(y + dy) % NY for dy in range(NY)]

    def hop(j):
        m = j // NY
        return (2 * (m % 2) - 1) * ((m + 1) // 2), j % NY

    def peer(j):
        dz, dy = hop(j)
        return planes[dz % NZ] * NY + columns[dy]

    def source(j):
        dz, dy = hop(j)
        return planes[-dz % NZ] * NY + columns[-dy % NY]

    def brick_copy(b):
        return pltpu.make_async_copy(volume.at[b], bricks.at[b], vol_sem.at[b])

    def tile_copy(chunk, j, land):
        return pltpu.make_async_remote_copy(
            src_ref=stage.at[chunk, peer(j)],
            dst_ref=landed.at[chunk, land],
            send_sem=send_sem.at[chunk, j],
            recv_sem=recv_sem.at[chunk, j],
            device_id={"tile": peer(j)},
            device_id_type=MESH,
        )

    def tag_copy(j, land):
        return pltpu.make_async_remote_copy(
            src_ref=tag_send.at[peer(j)],
            dst_ref=tag_land.at[land],
            send_sem=tag_out.at[j],
            recv_sem=tag_in.at[j],
            device_id={"tile": peer(j)},
            device_id_type=MESH,
        )

    def slab_copy(chunk, e, land):
        there = (slab + e) % SLABS
        return pltpu.make_async_remote_copy(
            src_ref=pieces.at[chunk, pl.ds(2 * there, 2)],
            dst_ref=bands.at[chunk, pl.ds(2 * land, 2)],
            send_sem=out_sem.at[chunk, e],
            recv_sem=in_sem.at[chunk, e],
            device_id={"depth": there},
            device_id_type=MESH,
        )

    def each(low, high, do, unroll=1):
        def step(i, _):
            do(i)
            return 0

        lax.fori_loop(low, high, step, 0, unroll=unroll)

    def every(do):
        for j in range(1, OWNERS):
            do(j)

    each(0, BRICKS, lambda b: brick_copy(b).start())
    barrier = pltpu.get_barrier_semaphore()
    every(
        lambda j: pl.semaphore_signal(barrier, inc=1, device_id={"tile": peer(j)}, device_id_type=MESH),
    )
    each(
        1,
        SLABS,
        lambda e: pl.semaphore_signal(
            barrier, inc=1, device_id={"depth": (slab + e) % SLABS}, device_id_type=MESH
        ),
    )
    coef = []
    for c in range(3):
        half = slope[c] * 0.5
        coef.append((half, -half * pivot[c]))
    wide[...] = jnp.zeros_like(wide)
    for view in range(2):
        wide[view, 0:ROWS, 0:COLS] = res[view]
        wide[view, ROWS : 2 * ROWS, COLS : 2 * COLS] = res[view]
    run[SLOTS] = jnp.zeros((4, RC, COLS), F32)
    table[...] = jnp.zeros_like(table)
    tag_land[tile] = tag_send[tile]
    pl.semaphore_wait(barrier, OWNERS + SLABS - 2)
    every(lambda j: tag_copy(j, tile).start())

    even, odd = (samples_a, thick_a), (samples_b, thick_b)
    brick_copy(0).wait()
    each(0, HALF, lambda pair: prepare(0, 0, pair, wide, bricks, *even))

    def render_and_send(chunk):
        def one(b):
            shared = (coef, res, wide, bricks, prints, sums)
            first, second = 2 * b, 2 * b + 1

            @pl.when(chunk == 0)
            def _():
                brick_copy(second).wait()

            march(first, chunk, second, chunk, *shared, even, odd)
            wrap = second // (BRICKS - 1)

            @pl.when((chunk == 0) & (b < BRICKS // 2 - 1))
            def _():
                brick_copy(second + 1).wait()

            march(
                second, chunk, (second + 1) % BRICKS, (chunk + wrap) % CHUNKS, *shared, odd, even
            )

        each(0, BRICKS // 2, one)

        def pick(o):
            one, two = item_of[2 * o], item_of[2 * o + 1]
            stage[chunk, o, 0 : 3 * RC, :] = prints[one]
            stage[chunk, o, 3 * RC : 6 * RC, :] = prints[two]
            stage[chunk, o, 6 * RC : BLOCK, :] = jnp.concatenate([sums[one], sums[two]], axis=0).astype(BF)

        each(0, OWNERS, pick)
        every(lambda j: tile_copy(chunk, j, tile).start())
        landed[chunk, tile] = stage[chunk, tile]

    each(0, CHUNKS, render_and_send)

    every(lambda j: tag_copy(j, source(j)).wait())
    depth_table(tag_land, table)
    scalars = pltpu.make_async_copy(table, table_s, table_sem)
    scalars.start()
    scalars.wait()

    def compose_and_send(chunk):
        every(lambda j: tile_copy(chunk, j, source(j)).wait())

        def keep(g):
            for i in range(8):
                src = g * 8 + i
                local[2 * src] = landed[chunk, src, 0 : 3 * RC, :]
                local[2 * src + 1] = landed[chunk, src, 3 * RC : 6 * RC, :]
            x = landed[chunk, pl.ds(g * 8, 8), 6 * RC : BLOCK, :].reshape(8 * RC, 2 * ROWS)
            for view in range(2):
                d = jnp.dot(x, wide[view], preferred_element_type=F32)
                depths[view, pl.ds(16 * g, 16)] = (d * (1.0 / 64.0)).reshape(16, HALF, 2 * COLS)

        each(0, OWNERS // 8, keep)

        def layer(p):
            slot = table_s[0, p]
            x = local[slot].astype(F32)
            d = depths[table_s[3, p], slot]
            base = run[table_s[1, p]]
            shade = jnp.exp(-base[3])
            run[p, 3] = base[3] + jnp.concatenate([d[:, :COLS], d[:, COLS:]], axis=0)
            for c in range(3):
                run[p, c] = base[c] + x[c * RC : (c + 1) * RC] * shade

        each(0, SLOTS, layer, 4)

        def close(t):
            pieces[chunk, t] = run[table_s[2, t]].astype(BF)

        each(0, TARGETS, close, 4)
        each(1, SLABS, lambda e: slab_copy(chunk, e, slab).start())
        bands[chunk, pl.ds(2 * slab, 2)] = pieces[chunk, pl.ds(2 * slab, 2)]

    each(0, CHUNKS, compose_and_send)

    def blend(chunk):
        each(1, SLABS, lambda e: slab_copy(chunk, e, (slab - e + SLABS) % SLABS).wait())
        band[...] = bands[chunk]
        rows = pl.ds(pl.multiple_of(chunk * RC, RC), RC)
        for view in range(2):
            front = jnp.zeros((RC, COLS), F32)
            acc = [front] * 3
            for j in range(SLABS):
                x = band[chain[view * SLABS + j] * 2 + view].astype(F32)
                shade = jnp.exp(-front)
                for c in range(3):
                    acc[c] = acc[c] + shade * x[c]
                front = front + x[3]
            for c in range(3):
                colour[view, c, 0, rows, :] = acc[c]
            light_out[view, 0, rows, :] = jnp.exp(-front)

    each(0, CHUNKS, blend)


def body(volume, resampler, slope, pivot, tile_owner, tile_cell, depth_order, slab_rank):
    ids = jnp.arange(ITEMS)
    owner = tile_owner.reshape(-1)
    same = (owner[None, :] == owner[:, None]) & (ids[None, :] < ids[:, None])
    place = owner * 2 + jnp.sum(same.astype(I32), axis=1)
    view = jnp.tile(jnp.arange(2, dtype=I32), BRICKS)
    tag = depth_order.T.reshape(-1) * TARGETS + tile_cell.reshape(-1) * 2 + view
    hit = place[None, :] == jnp.arange(SLOTS, dtype=I32)[:, None]
    item_of = jnp.sum(jnp.where(hit, ids[None, :], 0), axis=1)
    slot_tag = jnp.min(jnp.where(hit, tag[None, :], EMPTY), axis=1).reshape(OWNERS, 1, 2)
    tag_send = jnp.broadcast_to(jnp.pad(slot_tag, ((0, 0), (0, 0), (0, 126))), (OWNERS, 8, 128))
    slabs = jnp.arange(SLABS, dtype=I32)
    chain = jnp.sum(
        jnp.where(slab_rank[:, None, :] == slabs[None, :, None], slabs[None, None, :], 0), axis=2
    ).reshape(-1)
    smem = pl.BlockSpec(memory_space=pltpu.SMEM)
    vmem = pl.BlockSpec(memory_space=pltpu.VMEM)
    dma = pltpu.SemaphoreType.DMA
    return tuple(
        pl.pallas_call(
            kernel,
            in_specs=[smem, smem, smem, smem, vmem, vmem, pl.BlockSpec(memory_space=pl.ANY)],
            out_specs=[vmem, vmem],
            out_shape=[
                jax.ShapeDtypeStruct((2, 3, 1, ROWS, COLS), F32),
                jax.ShapeDtypeStruct((2, 1, ROWS, COLS), F32),
            ],
            scratch_shapes=[
                pltpu.VMEM((2, 2 * ROWS, 2 * COLS), BF),
                pltpu.VMEM((BRICKS, ROWS, ROWS, ROWS), BF),
                pltpu.VMEM((ITEMS, 3 * RC, COLS), BF),
                pltpu.VMEM((ITEMS, HALF, 2 * ROWS), F32),
                *SAMPLE_SCRATCH,
                pltpu.VMEM((HALF, 2 * ROWS), F32),
                pltpu.VMEM((HALF, 2 * ROWS), F32),
                pltpu.VMEM((CHUNKS, OWNERS, BLOCK, COLS), BF),
                pltpu.VMEM((CHUNKS, OWNERS, BLOCK, COLS), BF),
                pltpu.VMEM((SLOTS, 3 * RC, COLS), BF),
                pltpu.VMEM((2, SLOTS, HALF, 2 * COLS), F32),
                pltpu.VMEM((SLOTS + 1, 4, RC, COLS), F32),
                pltpu.VMEM((CHUNKS, TARGETS, 4, RC, COLS), BF),
                pltpu.VMEM((CHUNKS, TARGETS, 4, RC, COLS), BF),
                pltpu.VMEM((TARGETS, 4, RC, COLS), BF),
                pltpu.VMEM((OWNERS, 8, 128), I32),
                pltpu.VMEM((8, 128), I32),
                pltpu.SMEM((8, 128), I32),
                dma((BRICKS,)),
                dma((CHUNKS, OWNERS)),
                dma((CHUNKS, OWNERS)),
                dma((CHUNKS, SLABS)),
                dma((CHUNKS, SLABS)),
                dma((OWNERS,)),
                dma((OWNERS,)),
                dma(()),
            ],
            compiler_params=pltpu.CompilerParams(
                collective_id=0, has_side_effects=True, vmem_limit_bytes=52 << 20
            ),
            name="composite",
        )(item_of, chain, slope, pivot, tag_send, resampler, volume)
    )


def solution(mesh):
    in_specs = (
        P(("depth", "tile"), None, None, None),
        P(),
        P(),
        P(),
        P(("depth", "tile"), None),
        P(("depth", "tile"), None),
        P(None, ("depth", "tile")),
        P(),
    )
    out_specs = (P(None, None, "tile", "depth", None), P(None, "tile", "depth", None))
    return jax.shard_map(body, mesh=mesh, in_specs=in_specs, out_specs=out_specs, check_vma=False)
```
